32 devices in a mesh: energy: 8 (over z, x), atom: 4 (over y, core).
Axes of the slice: x: 2, y: 2, z: 4, core: 2. Of those that a mesh axis runs over, the one named last changes fastest.
Arguments:
- greens: bfloat16 [2, 64, 64, 256], P(None, ('energy', 'atom')), may hold values from -6 to 6
- coupling: bfloat16 [64, 8, 256], P('atom'), may hold values from -1.5 to 1.5
- neighbours: int32 [64, 8], P('atom'), may hold values from 0 to 63, as said below
- counts: int32 [64], P('atom'), may hold values from 4 to 8, as said below
- phonon_weights: float32 [2, 16], replicated, may hold values from 0.02 to 0.12
- offsets: int32 [16], replicated, may hold values from 1 to 8, as said below
Outputs:
- self_energy: bfloat16 [2, 64, 64, 256], P(None, 'energy', 'atom')
- phonon_self: float32 [64, 128], P('atom')
- current: float32 [64, 256], P(('energy', 'atom'))
The draws below stay inside these ranges and needn't reach their ends.
Inputs may be any that keep to these rules, and one draw needn't show every extreme that they name: `neighbours`: every entry of row a differs from a by 1 to 8; in every draw some entry lies exactly 8 from its atom. Atom a uses its first counts[a] listed neighbours; every draw holds an atom with 8 and one with 4. `offsets`: every draw holds a shift of 1 and a shift of 8.
All inputs are finite; a program needn't handle non-finite values.
Results may differ from the reference program's by a relative error of at most 0.0067.
Values may be sent and summed in bfloat16 or wider, within the bound.
A program may use at most 64 MiB of HBM per device.

```python
import math
import jax
import jax.numpy as jnp
from jax import lax

NO = 16
NB = 8
NW = 16
REACH = 8
NE = 64
NA = 64


def draw_neighbours(key, part):
    subkeys = jax.random.split(jax.random.fold_in(key, 11), 3)
    atom_ids = jnp.arange(NA, dtype=jnp.int32)[:, None]
    slot_ids = jnp.arange(NB, dtype=jnp.int32)[None, :]
    magnitude = jax.random.randint(subkeys[0], (NA, NB), 1, REACH + 1, dtype=jnp.int32)
    direction = jax.random.randint(subkeys[1], (NA, NB), 0, 2, dtype=jnp.int32) * 2 - 1
    chosen = jax.random.randint(subkeys[2], (), 0, NA, dtype=jnp.int32)
    magnitude = jnp.where((atom_ids == chosen) & (slot_ids == 0), REACH, magnitude)
    step_size = direction * magnitude
    target = atom_ids + step_size
    outside = (target < 0) | (target >= NA)
    return jnp.where(outside, atom_ids - step_size, target).astype(jnp.int32)


def draw_counts(key, part):
    subkeys = jax.random.split(jax.random.fold_in(key, 23), 3)
    atom_ids = jnp.arange(NA, dtype=jnp.int32)
    values = jax.random.randint(subkeys[0], (NA,), NB // 2, NB + 1, dtype=jnp.int32)
    first_pick = jax.random.randint(subkeys[1], (), 0, NA, dtype=jnp.int32)
    second_pick = (first_pick + 1 + jax.random.randint(subkeys[2], (), 0, NA - 1, dtype=jnp.int32)) % NA
    values = jnp.where(atom_ids == first_pick, NB, values)
    values = jnp.where(atom_ids == second_pick, NB // 2, values)
    return values.astype(jnp.int32)


def draw_offsets(key, part):
    subkeys = jax.random.split(jax.random.fold_in(key, 37), 3)
    freq_ids = jnp.arange(NW, dtype=jnp.int32)
    values = jax.random.randint(subkeys[0], (NW,), 1, REACH + 1, dtype=jnp.int32)
    first_pick = jax.random.randint(subkeys[1], (), 0, NW, dtype=jnp.int32)
    second_pick = (first_pick + 1 + jax.random.randint(subkeys[2], (), 0, NW - 1, dtype=jnp.int32)) % NW
    values = jnp.where(freq_ids == first_pick, REACH, values)
    values = jnp.where(freq_ids == second_pick, 1, values)
    return values.astype(jnp.int32)


def block_levels(key, dims, cuts, least, largest):
    loudness = 1.0
    for position, blocks in cuts:
        heights = jax.random.uniform(jax.random.fold_in(jax.random.fold_in(key, 6), position), (blocks,), jnp.float32, least / len(cuts), largest / len(cuts))
        loudness = loudness * jnp.repeat(jnp.exp(heights), dims[position] // blocks).reshape((-1,) + (1,) * (len(dims) - 1 - position))
    return loudness


def centred(own_key, dims, deviation, most, pieces=(), held_as=jnp.bfloat16):
    result = deviation * jax.random.normal(own_key, dims, jnp.float32)
    if pieces:
        result = result * block_levels(own_key, dims, pieces, -0.22, 0.18)
    return jnp.clip(result, -most, most).astype(held_as)


def setup_inputs(seed: int = 0) -> dict:
    keys = jax.random.split(jax.random.key(seed), 7)
    greens = centred(keys[0], (2, NE, NA, NO * NO), 1.0, 6.0, ((1, 32),))
    coupling = centred(keys[1], (NA, NB, NO * NO), NO ** -0.5, 1.5, ((0, 4),))
    neighbours = draw_neighbours(jax.random.fold_in(keys[6], 71), 0)
    counts = draw_counts(jax.random.fold_in(keys[6], 71), 0)
    phonon_weights = jnp.clip(jnp.exp(jax.random.uniform(keys[4], (2, NW), jnp.float32, math.log(0.02), math.log(0.12))), 0.02, 0.12)
    offsets = draw_offsets(jax.random.fold_in(keys[6], 71), 0)
    return dict(greens=greens, coupling=coupling, neighbours=neighbours, counts=counts, phonon_weights=phonon_weights, offsets=offsets)


def coefficients(phonon_weights, offsets):
    distance = jnp.arange(-REACH, REACH + 1, dtype=jnp.int32)[:, None]
    upward = (distance == offsets[None, :]).astype(jnp.float32)
    downward = (distance == -offsets[None, :]).astype(jnp.float32)
    emission = phonon_weights[0][None, :]
    absorption = phonon_weights[1][None, :]
    coef_less = lax.optimization_barrier(jnp.sum(emission * upward + absorption * downward, axis=1))
    coef_greater = lax.optimization_barrier(jnp.sum(emission * downward + absorption * upward, axis=1))
    return (coef_less.astype(jnp.bfloat16), coef_greater.astype(jnp.bfloat16))

def shift_mix(coef, field):
    padded = jnp.pad(field, ((REACH, REACH), (0, 0), (0, 0)))
    total = jnp.zeros(field.shape, jnp.float32)
    for offset in range(2 * REACH + 1):
        total = total + coef[offset].astype(jnp.float32) * padded[offset:offset + NE].astype(jnp.float32)
    return total.astype(jnp.bfloat16)

def reference(greens, coupling, neighbours, counts, phonon_weights, offsets):
    coef_less, coef_greater = coefficients(phonon_weights, offsets)
    mixed_less = shift_mix(coef_less, greens[0])
    mixed_greater = shift_mix(coef_greater, greens[1])
    padded_less = jnp.pad(greens[0], ((REACH, REACH), (0, 0), (0, 0)))
    scale_phonon = 1.0 / math.sqrt(NO * NO * NE)

    def slot_step(collected, slot_number):
        target = neighbours[:, slot_number]
        active = (slot_number < counts).astype(jnp.float32)
        matrix = coupling[:, slot_number].reshape(NA, NO, NO).astype(jnp.float32)
        gathered = jnp.stack([mixed_less[:, target], mixed_greater[:, target], greens[1][:, target]])
        gathered = gathered.reshape(3, NE, NA, NO, NO).astype(jnp.float32)
        left_half = jnp.einsum('aij,seajk->seaik', matrix, gathered)
        left_half = lax.optimization_barrier(left_half.astype(jnp.bfloat16)).astype(jnp.float32)
        sandwich = jnp.einsum('seaik,alk->seail', left_half, matrix).reshape(3, NE, NA, NO * NO)
        collected = collected + sandwich[:2] * active[None, None, :, None]
        bubble = lax.optimization_barrier(sandwich[2].astype(jnp.bfloat16)).astype(jnp.float32)
        phonon_terms = []
        for frequency in range(NW):
            start_row = (REACH + offsets[frequency]).astype(jnp.int32)
            shifted = lax.dynamic_slice_in_dim(padded_less, start_row, NE, 0).astype(jnp.float32)
            phonon_terms.append(lax.optimization_barrier(jnp.sum(bubble * shifted, axis=(0, 2))))
        return (collected, jnp.stack(phonon_terms) * (active * scale_phonon)[None, :])
    initial = jnp.zeros((2, NE, NA, NO * NO), jnp.float32)
    collected, terms = lax.scan(slot_step, initial, jnp.arange(NB, dtype=jnp.int32))
    self_energy = collected.astype(jnp.bfloat16)
    phonon_self = jnp.transpose(terms, (2, 0, 1)).reshape(NA, NB * NW)
    sigma = lax.optimization_barrier(self_energy).astype(jnp.float32).reshape(2, NE, NA, NO, NO)
    green_blocks = greens.astype(jnp.float32).reshape(2, NE, NA, NO, NO)
    gain = jnp.einsum('eaij,eajk->eik', sigma[1], green_blocks[0])
    loss = jnp.einsum('eaij,eajk->eik', sigma[0], green_blocks[1])
    current = (gain - loss).reshape(NE, NO * NO) / math.sqrt(NO * NA)
    return (self_energy, phonon_self, current)
```

```python
import functools
import math

import jax
import jax.numpy as jnp
from jax import lax
from jax.experimental import pallas as pl
from jax.experimental.pallas import tpu as pltpu
from jax.sharding import PartitionSpec as P

NO = 16
REACH = 8
LANES = 128
MESH = pl.DeviceIdType.MESH


def iota(shape, dim):
    return lax.broadcasted_iota(jnp.int32, shape, dim)


def kernel(
    n_e, n_a,
    greens, coupling, neighbours, counts, weights, offsets,
    sigma_out, phonon_out, current_out,
    spread, sendbuf, recv, framed, left, right, kron, sources,
    sums, inter, pre, mine_p, got_p, mine_c, got_c,
    send_sem, recv_sem, own_sem, psend, precv, csend, crecv,
):
    _, rows, all_atoms, cells = greens.shape
    atoms, slots = neighbours.shape
    edges = atoms * slots
    width = n_a * rows
    span = width + 2 * REACH
    planes = 2 * rows
    window = atoms + 2 * REACH
    chunks = window // REACH
    halves = cells // LANES
    line = 2 * window
    ei = lax.axis_index("energy")
    ai = lax.axis_index("atom")
    lower = ei > 0
    upper = ei < n_e - 1
    f32, bf16 = jnp.float32, jnp.bfloat16

    def ok(d):
        return {-1: lower, 1: upper}.get(d)

    def guarded(d, body):
        if d == 0:
            body()
        else:
            pl.when(ok(d))(body)

    barrier = pltpu.get_barrier_semaphore()

    def greet(e, a):
        pl.semaphore_signal(barrier, inc=1, device_id=(e, a), device_id_type=MESH)

    for d in (-1, 0, 1):
        for k in range(n_a):
            if d or k:
                guarded(d, lambda d=d, k=k: greet(ei + d, lax.rem(ai + k, n_a)))

    def greet_far(k, carry):
        other = lax.rem(ei + k, n_e)
        pl.when((other != ei - 1) & (other != ei + 1))(lambda: greet(other, ai))
        return carry

    lax.fori_loop(1, n_e, greet_far, 0)

    stretch = 2 * all_atoms
    for plane in range(planes):
        for h in range(halves):
            spread[pl.ds(plane * stretch + h, all_atoms, stride=2), :] = greens[
                plane // rows, plane % rows, :, h * LANES:(h + 1) * LANES
            ].astype(f32)
    none = jnp.zeros((2 * REACH, LANES), bf16)
    for plane in range(planes):
        sendbuf[plane, 0] = none
        sendbuf[plane, all_atoms // REACH + 1] = none
        sendbuf[plane, 1:all_atoms // REACH + 1] = (
            spread[plane * stretch:(plane + 1) * stretch, :]
            .astype(bf16).reshape(all_atoms // REACH, 2 * REACH, LANES)
        )

    near = lower.astype(jnp.int32) + upper.astype(jnp.int32)
    pl.semaphore_wait(barrier, n_a - 1 + n_a * near + (n_e - 1 - near))

    step = atoms // REACH

    def block_copy(d, k):
        other = lax.rem(ai + k, n_a)
        slot = (1 - d) * n_a + ai
        return pltpu.make_async_remote_copy(
            src_ref=sendbuf.at[:, pl.ds(step * other, chunks)],
            dst_ref=recv.at[slot],
            send_sem=send_sem.at[(d + 1) * n_a + k],
            recv_sem=recv_sem.at[slot],
            device_id=(ei + d, other),
            device_id_type=MESH,
        )

    for k in range(n_a - 1, -1, -1):
        for d in (-1, 1, 0):
            if d or k:
                guarded(d, lambda d=d, k=k: block_copy(d, k).start())
    own = pltpu.make_async_copy(
        sendbuf.at[:, pl.ds(step * ai, chunks)], recv.at[n_a + ai], own_sem
    )
    own.start()

    def clear(first):
        for k in range(n_a):
            recv[first + k] = jnp.zeros(recv.shape[1:], bf16)

    pl.when(jnp.logical_not(lower))(lambda: clear(0))
    pl.when(jnp.logical_not(upper))(lambda: clear(2 * n_a))

    big_row, big_col = iota((cells, cells), 0), iota((cells, cells), 1)
    same_block = (big_row // NO == big_col // NO).astype(f32).astype(bf16)
    same_place = (big_row // NO == big_col % NO).astype(f32).astype(bf16)
    flat = coupling[...].reshape(edges, cells).astype(f32)
    place = iota((edges, cells), 1) % NO

    def expand(j, carry):
        picked = jnp.where(place == j, flat, 0.0).astype(bf16)
        one = jnp.dot(picked, same_block, preferred_element_type=f32)
        two = jnp.dot(picked, same_place, preferred_element_type=f32)
        for h in range(halves):
            at = pl.ds(pl.multiple_of((h * NO + j) * edges, edges), edges)
            left[at, :] = one[:, h * LANES:(h + 1) * LANES]
            right[at, :] = two[:, h * LANES:(h + 1) * LANES]
        return carry

    lax.fori_loop(0, NO, expand, 0)

    def product(edge, carry):
        for h in range(halves):
            block = right[pl.ds(h * NO * edges + edge, NO, stride=edges), :]
            for j in range(NO):
                row = left[pl.ds((h * NO + j) * edges + edge, 1), :]
                kron[edge, j * NO:(j + 1) * NO, h * LANES:(h + 1) * LANES] = (
                    jnp.broadcast_to(row, (NO, LANES)) * block
                ).astype(bf16)
        return carry

    lax.fori_loop(0, edges, product, 0)

    shape = (6 * width, 2 * span)
    row, col = iota(shape, 0), iota(shape, 1)
    kind = row // width
    half = (col // rows) % 2
    energy = (col // planes) * rows + col % rows
    distance = energy - row % width - REACH
    shift = jnp.where(kind == 0, distance, -distance)
    coef = jnp.zeros(shape, f32)
    for w in range(offsets.shape[0]):
        coef = coef + jnp.where(shift == offsets[w], weights[0, w], 0.0)
        coef = coef + jnp.where(shift == -offsets[w], weights[1, w], 0.0)
    middle = jnp.where((kind == 2) & (half == 1) & (distance == 0), 1.0, 0.0)
    above = jnp.where((kind >= 4) & (half == 0) & (energy - REACH == row - 4 * width), 1.0, 0.0)
    table = jnp.where((kind < 2) & (kind == half), coef, middle + above).astype(bf16)

    own.wait()
    for d in (-1, 0, 1):
        for k in range(n_a):
            if d or k:
                def arrive(d=d, k=k):
                    slot = (d + 1) * n_a + lax.rem(ai + k, n_a)
                    pltpu.make_async_remote_copy(
                        src_ref=sendbuf.at[:, pl.ds(0, chunks)],
                        dst_ref=recv.at[slot],
                        send_sem=send_sem.at[(d + 1) * n_a + k],
                        recv_sem=recv_sem.at[slot],
                        device_id=(ei + d, lax.rem(ai + k, n_a)),
                        device_id_type=MESH,
                    ).wait()
                guarded(d, arrive)

    def widen(position, carry):
        for plane in range(planes):
            at = pl.multiple_of((position * planes + plane) * line, line)
            framed[pl.ds(at, line), :] = recv[position, plane].reshape(line, LANES).astype(f32)
        return carry

    lax.fori_loop(0, 3 * n_a, widen, 0)

    def mix(t, carry):
        for h in range(halves):
            column = framed[pl.ds(2 * t + h, 2 * span, stride=line), :].astype(bf16)
            sources[t, :, h * LANES:(h + 1) * LANES] = jnp.dot(
                table, column, preferred_element_type=f32
            ).astype(bf16)
        return carry

    lax.fori_loop(0, window, mix, 0)

    first = ai * atoms - REACH
    both = 2 * width

    def atom_step(a, carry):
        total = jnp.zeros((both, cells), f32)
        bubbles = []
        for n in range(slots):
            place = jnp.clip(neighbours[a, n] - first, 0, window - 1)
            mixed = sources[place, 0:4 * width, :]
            result = jnp.dot(mixed, kron[a * slots + n], preferred_element_type=f32)
            live = jnp.where(n < counts[a], 1.0, 0.0)
            total = total + result[:both] * live
            bubbles.append(result[both:both + width])
        bubble = jnp.concatenate(bubbles, axis=0).astype(bf16)
        inter[pl.ds(pl.multiple_of(a * slots * width, slots * width), slots * width), 0:both] = (
            lax.dot_general(
                bubble, sources[REACH + a, 4 * width:6 * width, :],
                (((1,), (1,)), ((), ())), preferred_element_type=f32,
            )
        )
        for h in range(halves):
            sums[pl.ds(h * both * atoms + a, both, stride=atoms), :] = total[
                :, h * LANES:(h + 1) * LANES
            ]
        return carry

    inter[...] = jnp.zeros(inter.shape, f32)
    lax.fori_loop(0, atoms, atom_step, 0)

    by_shift = jnp.zeros((edges, LANES), f32)
    for e in range(width):
        part = inter[pl.ds(e, edges, stride=width), :]
        by_shift = by_shift + pltpu.roll(part, (LANES - e - 1) % LANES, 1)
    mine_p[...] = by_shift.T[0:REACH, :]

    def phonon_copy(k):
        other = lax.rem(ei + k, n_e)
        return pltpu.make_async_remote_copy(
            src_ref=mine_p, dst_ref=got_p.at[ei],
            send_sem=psend.at[k], recv_sem=precv.at[ei],
            device_id=(other, ai), device_id_type=MESH,
        )

    def phonon_send(k, carry):
        phonon_copy(k).start()
        return carry

    lax.fori_loop(1, n_e, phonon_send, 0)

    place = iota((NO, cells), 1) % NO
    for e in range(width):
        sig, gre = [], []
        for s in (1, 0):
            parts = []
            for h in range(halves):
                at = (h * both + s * width + e) * atoms
                value = sums[at:at + atoms, :].astype(bf16)
                sigma_out[s, e, :, h * LANES:(h + 1) * LANES] = value
                parts.append(value)
            sig.append(jnp.concatenate(parts, axis=1))
        for g in range(2):
            base = ((n_a + e // rows) * planes + g * rows + e % rows) * line + 2 * REACH
            gre.append(jnp.concatenate(
                [framed[pl.ds(base + h, atoms, stride=2), :].astype(bf16) for h in range(halves)],
                axis=1,
            ))
        outer = lax.dot_general(
            jnp.concatenate(gre, axis=0), jnp.concatenate([sig[0], -sig[1]], axis=0),
            (((0,), (0,)), ((), ())), preferred_element_type=f32,
        )
        chosen = jnp.zeros((NO, cells), f32)
        for j in range(NO):
            chosen = jnp.where(place == j, outer[j * NO:(j + 1) * NO, :], chosen)
        pre[e * NO:(e + 1) * NO, :] = chosen
    value = pre[...]
    high = value.astype(bf16)
    low = (value - high.astype(f32)).astype(bf16)
    wide = jnp.dot(high, same_block, preferred_element_type=f32)
    wide = wide + jnp.dot(low, same_block, preferred_element_type=f32)
    keep = iota((width * NO, cells), 0) % NO == iota((width * NO, cells), 1) % NO
    wide = jnp.where(keep, wide, 0.0).reshape(width, NO, cells)
    share = jnp.sum(wide, axis=1) * (1.0 / math.sqrt(NO * all_atoms))
    mine_c[...] = share

    def current_copy(k):
        other = lax.rem(ai + k, n_a)
        return pltpu.make_async_remote_copy(
            src_ref=mine_c, dst_ref=got_c.at[ai],
            send_sem=csend.at[k], recv_sem=crecv.at[ai],
            device_id=(ei, other), device_id_type=MESH,
        )

    for k in range(1, n_a):
        current_copy(k).start()

    def phonon_wait(k, total):
        slot = lax.rem(ei + k, n_e)
        pltpu.make_async_remote_copy(
            src_ref=mine_p, dst_ref=got_p.at[slot],
            send_sem=psend.at[k], recv_sem=precv.at[slot],
            device_id=(slot, ai), device_id_type=MESH,
        ).wait()
        return total + got_p[slot]

    found = lax.fori_loop(1, n_e, phonon_wait, mine_p[...])
    count_w = offsets.shape[0]
    lanes = slots * count_w
    frequency = iota((REACH, lanes), 1) % count_w
    wanted = jnp.zeros((REACH, lanes), jnp.int32)
    for w in range(count_w):
        wanted = jnp.where(frequency == w, offsets[w], wanted)
    select = (wanted - 1 == iota((REACH, lanes), 0)).astype(f32)
    tall = found.T
    picked = jnp.zeros((edges, lanes), f32)
    for k in range(REACH):
        picked = picked + tall[:, k:k + 1] * select[k:k + 1, :]
    keep = iota((edges, lanes), 0) % slots == iota((edges, lanes), 1) // count_w
    picked = jnp.sum(jnp.where(keep, picked, 0.0).reshape(atoms, slots, lanes), axis=1)
    used = jnp.zeros((atoms, lanes), jnp.int32)
    which = iota((atoms, lanes), 0)
    for a in range(atoms):
        used = jnp.where(which == a, counts[a], used)
    live = iota((atoms, lanes), 1) // count_w < used
    phonon_out[...] = jnp.where(live, picked * (1.0 / math.sqrt(cells * width * n_e)), 0.0)

    total = mine_c[...]
    for k in range(1, n_a):
        slot = lax.rem(ai + k, n_a)
        pltpu.make_async_remote_copy(
            src_ref=mine_c, dst_ref=got_c.at[slot],
            send_sem=csend.at[k], recv_sem=crecv.at[slot],
            device_id=(ei, slot), device_id_type=MESH,
        ).wait()
        total = total + got_c[slot]
    own_rows = total[0:rows]
    for k in range(1, n_a):
        own_rows = jnp.where(ai == k, total[k * rows:(k + 1) * rows], own_rows)
    current_out[...] = own_rows


def shards(n_e, n_a, greens, coupling, neighbours, counts, phonon_weights, offsets):
    _, rows, all_atoms, cells = greens.shape
    atoms, slots = neighbours.shape
    edges = atoms * slots
    width = n_a * rows
    span = width + 2 * REACH
    window = atoms + 2 * REACH
    chunks = window // REACH
    f32, bf16 = jnp.float32, jnp.bfloat16
    halves = cells // LANES
    vmem = pl.BlockSpec(memory_space=pltpu.VMEM)
    smem = pl.BlockSpec(memory_space=pltpu.SMEM)
    dma = pltpu.SemaphoreType.DMA
    return pl.pallas_call(
        functools.partial(kernel, n_e, n_a),
        out_shape=(
            jax.ShapeDtypeStruct((2, width, atoms, cells), bf16),
            jax.ShapeDtypeStruct((atoms, slots * offsets.shape[0]), f32),
            jax.ShapeDtypeStruct((rows, cells), f32),
        ),
        in_specs=[vmem, vmem, smem, smem, smem, smem],
        out_specs=(vmem, vmem, vmem),
        scratch_shapes=[
            pltpu.VMEM((2 * rows * 2 * all_atoms, LANES), f32),
            pltpu.VMEM((2 * rows, all_atoms // REACH + 2, 2 * REACH, LANES), bf16),
            pltpu.VMEM((3 * n_a, 2 * rows, chunks, 2 * REACH, LANES), bf16),
            pltpu.VMEM((2 * span * 2 * window, LANES), f32),
            pltpu.VMEM((halves * NO * edges, LANES), f32),
            pltpu.VMEM((halves * NO * edges, LANES), f32),
            pltpu.VMEM((edges, cells, cells), bf16),
            pltpu.VMEM((window, 6 * width, cells), bf16),
            pltpu.VMEM((halves * 2 * width * atoms, LANES), f32),
            pltpu.VMEM((edges * width, LANES), f32),
            pltpu.VMEM((width * NO, cells), f32),
            pltpu.VMEM((REACH, edges), f32),
            pltpu.VMEM((n_e, REACH, edges), f32),
            pltpu.VMEM((width, cells), f32),
            pltpu.VMEM((n_a, width, cells), f32),
            dma((3 * n_a,)), dma((3 * n_a,)), dma,
            dma((n_e,)), dma((n_e,)), dma((n_a,)), dma((n_a,)),
        ],
        compiler_params=pltpu.CompilerParams(
            collective_id=0, has_side_effects=True, vmem_limit_bytes=48 * 1024 * 1024
        ),
    )(greens, coupling, neighbours, counts, phonon_weights, offsets)


def solution(mesh):
    placed = (
        P(None, ("energy", "atom"), None, None),
        P("atom", None, None),
        P("atom", None),
        P("atom"),
        P(),
        P(),
    )
    return jax.shard_map(
        functools.partial(shards, mesh.shape["energy"], mesh.shape["atom"]),
        mesh=mesh,
        in_specs=placed,
        out_specs=(P(None, "energy", "atom", None), P("atom", None), P(("energy", "atom"), None)),
        check_vma=False,
    )
```

```python
import functools
import math

import jax
import jax.numpy as jnp
from jax import lax
from jax.experimental import pallas as pl
from jax.experimental.pallas import tpu as pltpu
from jax.sharding import PartitionSpec as P

NO = 16
REACH = 8
LANES = 128
MESH = pl.DeviceIdType.MESH


def iota(shape, dim):
    return lax.broadcasted_iota(jnp.int32, shape, dim)


def kernel(
    n_e, n_a,
    greens, coupling, neighbours, counts, weights, offsets,
    sigma_out, phonon_out, current_out,
    local_coupling, recv, framed, left, right, kron, sources, higher,
    sums, inter, pre, mine_p, got_p, mine_c, got_c,
    send_sem, recv_sem, own_sem, esend, erecv, psend, precv, csend, crecv,
):
    _, rows, all_atoms, cells = greens.shape
    slots, atoms = neighbours.shape
    edges = atoms * slots
    width = n_a * rows
    span = width + 2 * REACH
    planes = 2 * rows
    window = atoms + 2 * REACH
    halves = cells // LANES
    line = halves * atoms
    ei = lax.axis_index("energy")
    ai = lax.axis_index("atom")
    lower = ei > 0
    upper = ei < n_e - 1
    f32, bf16 = jnp.float32, jnp.bfloat16

    def ok(d):
        return {-1: lower, 1: upper}.get(d)

    def guarded(d, body):
        if d == 0:
            body()
        else:
            pl.when(ok(d))(body)

    barrier = pltpu.get_barrier_semaphore()

    def greet(e, a):
        pl.semaphore_signal(barrier, inc=1, device_id=(e, a), device_id_type=MESH)

    for d in (-1, 0, 1):
        for k in range(n_a):
            if d or k:
                guarded(d, lambda d=d, k=k: greet(ei + d, lax.rem(ai + k, n_a)))

    def greet_far(k, carry):
        other = lax.rem(ei + k, n_e)
        pl.when((other != ei - 1) & (other != ei + 1))(lambda: greet(other, ai))
        return carry

    lax.fori_loop(1, n_e, greet_far, 0)

    near = lower.astype(jnp.int32) + upper.astype(jnp.int32)
    pl.semaphore_wait(barrier, n_a - 1 + n_a * near + (n_e - 1 - near))

    coupling_copy = pltpu.make_async_copy(coupling, local_coupling, own_sem.at[1])
    coupling_copy.start()

    def part(other):
        return greens.at[:, :, pl.ds(pl.multiple_of(other * atoms, atoms), atoms), :]

    def block_copy(d, k):
        other = lax.rem(ai + k, n_a)
        slot = (1 - d) * n_a + ai
        return pltpu.make_async_remote_copy(
            src_ref=part(other),
            dst_ref=recv.at[slot],
            send_sem=send_sem.at[(d + 1) * n_a + k],
            recv_sem=recv_sem.at[slot],
            device_id=(ei + d, other),
            device_id_type=MESH,
        )

    for k in range(n_a - 1, -1, -1):
        for d in (-1, 1, 0):
            if d or k:
                guarded(d, lambda d=d, k=k: block_copy(d, k).start())
    own = pltpu.make_async_copy(part(ai), recv.at[n_a + ai], own_sem.at[0])
    own.start()

    def clear(first):
        for k in range(n_a):
            recv[first + k] = jnp.zeros(recv.shape[1:], bf16)

    pl.when(jnp.logical_not(lower))(lambda: clear(0))
    pl.when(jnp.logical_not(upper))(lambda: clear(2 * n_a))

    big_row, big_col = iota((cells, cells), 0), iota((cells, cells), 1)
    same_block = (big_row // NO == big_col // NO).astype(f32).astype(bf16)
    same_place = (big_row // NO == big_col % NO).astype(f32).astype(bf16)
    coupling_copy.wait()
    flat = local_coupling[...].reshape(edges, cells).astype(f32)
    place = iota((edges, cells), 1) % NO

    def expand(j, carry):
        picked = jnp.where(place == j, flat, 0.0).astype(bf16)
        one = jnp.dot(picked, same_block, preferred_element_type=f32)
        two = jnp.dot(picked, same_place, preferred_element_type=f32)
        for h in range(halves):
            at = pl.ds(pl.multiple_of((h * NO + j) * edges, edges), edges)
            left[at, :] = one[:, h * LANES:(h + 1) * LANES]
            right[at, :] = two[:, h * LANES:(h + 1) * LANES]
        return carry

    lax.fori_loop(0, NO, expand, 0, unroll=4)

    def product(edge, carry):
        for h in range(halves):
            block = right[pl.ds(h * NO * edges + edge, NO, stride=edges), :]
            for j in range(NO):
                row = left[pl.ds((h * NO + j) * edges + edge, 1), :]
                kron[edge, j * NO:(j + 1) * NO, h * LANES:(h + 1) * LANES] = (
                    jnp.broadcast_to(row, (NO, LANES)) * block
                ).astype(bf16)
        return carry

    early = edges * 5 // 8
    lax.fori_loop(0, early, product, 0, unroll=4)

    shape = (6 * width, 2 * span)
    row, col = iota(shape, 0), iota(shape, 1)
    kind = row // width
    half = (col // rows) % 2
    energy = (col // planes) * rows + col % rows
    distance = energy - row % width - REACH
    shift = jnp.where(kind == 0, distance, -distance)
    coef = jnp.zeros(shape, f32)
    for w in range(offsets.shape[0]):
        coef = coef + jnp.where(shift == offsets[w], weights[0, w], 0.0)
        coef = coef + jnp.where(shift == -offsets[w], weights[1, w], 0.0)
    middle = jnp.where((kind == 2) & (half == 1) & (distance == 0), 1.0, 0.0)
    above = jnp.where((kind >= 4) & (half == 0) & (energy - REACH == row - 4 * width), 1.0, 0.0)
    table = jnp.where((kind < 2) & (kind == half), coef, middle + above).astype(bf16)

    own.wait()
    for d in (-1, 0, 1):
        for k in range(n_a):
            if d or k:
                def arrive(d=d, k=k):
                    slot = (d + 1) * n_a + lax.rem(ai + k, n_a)
                    pltpu.make_async_remote_copy(
                        src_ref=part(0),
                        dst_ref=recv.at[slot],
                        send_sem=send_sem.at[(d + 1) * n_a + k],
                        recv_sem=recv_sem.at[slot],
                        device_id=(ei + d, lax.rem(ai + k, n_a)),
                        device_id_type=MESH,
                    ).wait()
                guarded(d, arrive)

    def widen(position, carry):
        for plane in range(planes):
            value = recv[position, plane // rows, plane % rows].astype(f32)
            for h in range(halves):
                at = pl.multiple_of((position * planes + plane) * line + h * atoms, atoms)
                framed[pl.ds(at, atoms), :] = value[:, h * LANES:(h + 1) * LANES]
        return carry

    lax.fori_loop(0, 3 * n_a, widen, 0)

    def mix(t, carry):
        column = jnp.concatenate(
            [framed[pl.ds(h * atoms + t, 2 * span, stride=line), :] for h in range(halves)], axis=1
        ).astype(bf16)
        mixed = jnp.dot(table, column, preferred_element_type=f32).astype(bf16)
        sources[REACH + t] = mixed[0:4 * width]
        higher[t] = mixed[4 * width:]
        return carry

    has_left, has_right = ai > 0, ai < n_a - 1

    def edge_copy(side):
        start, landing = (REACH, REACH + atoms) if side == 0 else (atoms, 0)
        return pltpu.make_async_remote_copy(
            src_ref=sources.at[pl.ds(start, REACH)],
            dst_ref=sources.at[pl.ds(landing, REACH)],
            send_sem=esend.at[side],
            recv_sem=erecv.at[side],
            device_id=(ei, ai - 1 + 2 * side),
            device_id_type=MESH,
        )

    lax.fori_loop(0, REACH, mix, 0, unroll=4)
    pl.when(has_left)(lambda: edge_copy(0).start())
    lax.fori_loop(REACH, atoms, mix, 0, unroll=4)
    pl.when(has_right)(lambda: edge_copy(1).start())
    lax.fori_loop(early, edges, product, 0, unroll=4)
    pl.when(has_left)(lambda: edge_copy(0).wait_send())
    pl.when(has_right)(lambda: edge_copy(1).wait_send())
    pl.when(has_right)(lambda: edge_copy(0).wait_recv())
    pl.when(has_left)(lambda: edge_copy(1).wait_recv())

    first = ai * atoms - REACH
    both = 2 * width

    def atom_step(a, carry):
        total = jnp.zeros((both, cells), f32)
        bubbles = []
        for n in range(slots):
            place = jnp.clip(neighbours[n, a] - first, 0, window - 1)
            mixed = sources[place]
            result = jnp.dot(mixed, kron[a * slots + n], preferred_element_type=f32)
            live = jnp.where(n < counts[a], 1.0, 0.0)
            total = total + result[:both] * live
            bubbles.append(result[both:both + width])
        bubble = jnp.concatenate(bubbles, axis=0).astype(bf16)
        inter[pl.ds(pl.multiple_of(a * slots * width, slots * width), slots * width), 0:both] = (
            lax.dot_general(
                bubble, higher[a],
                (((1,), (1,)), ((), ())), preferred_element_type=f32,
            )
        )
        for h in range(halves):
            sums[pl.ds(h * both * atoms + a, both, stride=atoms), :] = total[
                :, h * LANES:(h + 1) * LANES
            ]
        return carry

    inter[...] = jnp.zeros(inter.shape, f32)
    lax.fori_loop(0, atoms, atom_step, 0, unroll=4)

    by_shift = jnp.zeros((edges, LANES), f32)
    for e in range(width):
        part = inter[pl.ds(e, edges, stride=width), :]
        by_shift = by_shift + pltpu.roll(part, (LANES - e - 1) % LANES, 1)
    mine_p[...] = by_shift.T[0:REACH, :]

    def phonon_copy(k):
        other = lax.rem(ei + k, n_e)
        return pltpu.make_async_remote_copy(
            src_ref=mine_p, dst_ref=got_p.at[ei],
            send_sem=psend.at[k], recv_sem=precv.at[ei],
            device_id=(other, ai), device_id_type=MESH,
        )

    def phonon_send(k, carry):
        phonon_copy(k).start()
        return carry

    lax.fori_loop(1, n_e, phonon_send, 0)

    place = iota((NO, cells), 1) % NO
    for e in range(width):
        sig, gre = [], []
        for s in (1, 0):
            parts = []
            for h in range(halves):
                at = (h * both + s * width + e) * atoms
                value = sums[at:at + atoms, :].astype(bf16)
                sigma_out[s, e, :, h * LANES:(h + 1) * LANES] = value
                parts.append(value)
            sig.append(jnp.concatenate(parts, axis=1))
        for g in range(2):
            base = ((n_a + e // rows) * planes + g * rows + e % rows) * line
            gre.append(jnp.concatenate(
                [framed[base + h * atoms:base + (h + 1) * atoms, :].astype(bf16) for h in range(halves)],
                axis=1,
            ))
        outer = lax.dot_general(
            jnp.concatenate(gre, axis=0), jnp.concatenate([sig[0], -sig[1]], axis=0),
            (((0,), (0,)), ((), ())), preferred_element_type=f32,
        )
        chosen = jnp.zeros((NO, cells), f32)
        for j in range(NO):
            chosen = jnp.where(place == j, outer[j * NO:(j + 1) * NO, :], chosen)
        pre[e * NO:(e + 1) * NO, :] = chosen
    value = pre[...]
    high = value.astype(bf16)
    low = (value - high.astype(f32)).astype(bf16)
    wide = jnp.dot(high, same_block, preferred_element_type=f32)
    wide = wide + jnp.dot(low, same_block, preferred_element_type=f32)
    keep = iota((width * NO, cells), 0) % NO == iota((width * NO, cells), 1) % NO
    wide = jnp.where(keep, wide, 0.0).reshape(width, NO, cells)
    share = jnp.sum(wide, axis=1) * (1.0 / math.sqrt(NO * all_atoms))
    mine_c[...] = share

    def current_copy(k):
        other = lax.rem(ai + k, n_a)
        return pltpu.make_async_remote_copy(
            src_ref=mine_c, dst_ref=got_c.at[ai],
            send_sem=csend.at[k], recv_sem=crecv.at[ai],
            device_id=(ei, other), device_id_type=MESH,
        )

    for k in range(1, n_a):
        current_copy(k).start()

    def phonon_wait(k, total):
        slot = lax.rem(ei + k, n_e)
        pltpu.make_async_remote_copy(
            src_ref=mine_p, dst_ref=got_p.at[slot],
            send_sem=psend.at[k], recv_sem=precv.at[slot],
            device_id=(slot, ai), device_id_type=MESH,
        ).wait()
        return total + got_p[slot]

    found = lax.fori_loop(1, n_e, phonon_wait, mine_p[...])
    count_w = offsets.shape[0]
    lanes = slots * count_w
    frequency = iota((REACH, lanes), 1) % count_w
    wanted = jnp.zeros((REACH, lanes), jnp.int32)
    for w in range(count_w):
        wanted = jnp.where(frequency == w, offsets[w], wanted)
    select = (wanted - 1 == iota((REACH, lanes), 0)).astype(f32)
    tall = found.T
    picked = jnp.zeros((edges, lanes), f32)
    for k in range(REACH):
        picked = picked + tall[:, k:k + 1] * select[k:k + 1, :]
    keep = iota((edges, lanes), 0) % slots == iota((edges, lanes), 1) // count_w
    picked = jnp.sum(jnp.where(keep, picked, 0.0).reshape(atoms, slots, lanes), axis=1)
    used = jnp.zeros((atoms, lanes), jnp.int32)
    which = iota((atoms, lanes), 0)
    for a in range(atoms):
        used = jnp.where(which == a, counts[a], used)
    live = iota((atoms, lanes), 1) // count_w < used
    phonon_out[...] = jnp.where(live, picked * (1.0 / math.sqrt(cells * width * n_e)), 0.0)

    total = mine_c[...]
    for k in range(1, n_a):
        slot = lax.rem(ai + k, n_a)
        pltpu.make_async_remote_copy(
            src_ref=mine_c, dst_ref=got_c.at[slot],
            send_sem=csend.at[k], recv_sem=crecv.at[slot],
            device_id=(ei, slot), device_id_type=MESH,
        ).wait()
        total = total + got_c[slot]
    own_rows = total[0:rows]
    for k in range(1, n_a):
        own_rows = jnp.where(ai == k, total[k * rows:(k + 1) * rows], own_rows)
    current_out[...] = own_rows


def shards(n_e, n_a, greens, coupling, neighbours, counts, phonon_weights, offsets):
    _, rows, all_atoms, cells = greens.shape
    atoms, slots = neighbours.shape
    edges = atoms * slots
    width = n_a * rows
    span = width + 2 * REACH
    window = atoms + 2 * REACH
    f32, bf16 = jnp.float32, jnp.bfloat16
    halves = cells // LANES
    vmem = pl.BlockSpec(memory_space=pltpu.VMEM)
    hbm = pl.BlockSpec(memory_space=pltpu.HBM)
    smem = pl.BlockSpec(memory_space=pltpu.SMEM)
    dma = pltpu.SemaphoreType.DMA
    return pl.pallas_call(
        functools.partial(kernel, n_e, n_a),
        out_shape=(
            jax.ShapeDtypeStruct((2, width, atoms, cells), bf16),
            jax.ShapeDtypeStruct((atoms, slots * offsets.shape[0]), f32),
            jax.ShapeDtypeStruct((rows, cells), f32),
        ),
        in_specs=[hbm, hbm, smem, smem, smem, smem],
        out_specs=(vmem, vmem, vmem),
        scratch_shapes=[
            pltpu.VMEM(coupling.shape, bf16),
            pltpu.VMEM((3 * n_a, 2, rows, atoms, cells), bf16),
            pltpu.VMEM((2 * span * halves * atoms, LANES), f32),
            pltpu.VMEM((halves * NO * edges, LANES), f32),
            pltpu.VMEM((halves * NO * edges, LANES), f32),
            pltpu.VMEM((edges, cells, cells), bf16),
            pltpu.VMEM((window, 4 * width, cells), bf16),
            pltpu.VMEM((atoms, 2 * width, cells), bf16),
            pltpu.VMEM((halves * 2 * width * atoms, LANES), f32),
            pltpu.VMEM((edges * width, LANES), f32),
            pltpu.VMEM((width * NO, cells), f32),
            pltpu.VMEM((REACH, edges), f32),
            pltpu.VMEM((n_e, REACH, edges), f32),
            pltpu.VMEM((width, cells), f32),
            pltpu.VMEM((n_a, width, cells), f32),
            dma((3 * n_a,)), dma((3 * n_a,)), dma((2,)), dma((2,)), dma((2,)),
            dma((n_e,)), dma((n_e,)), dma((n_a,)), dma((n_a,)),
        ],
        compiler_params=pltpu.CompilerParams(
            collective_id=0, has_side_effects=True, vmem_limit_bytes=63 * 1024 * 1024
        ),
    )(greens, coupling, neighbours.T, counts, phonon_weights, offsets)


def solution(mesh):
    placed = (
        P(None, ("energy", "atom"), None, None),
        P("atom", None, None),
        P("atom", None),
        P("atom"),
        P(),
        P(),
    )
    return jax.shard_map(
        functools.partial(shards, mesh.shape["energy"], mesh.shape["atom"]),
        mesh=mesh,
        in_specs=placed,
        out_specs=(P(None, "energy", "atom", None), P("atom", None), P(("energy", "atom"), None)),
        check_vma=False,
    )
```

```python
import functools
import math

import jax
import jax.numpy as jnp
from jax import lax
from jax.experimental import pallas as pl
from jax.experimental.pallas import tpu as pltpu
from jax.sharding import PartitionSpec as P

NO = 16
REACH = 8
LANES = 128
MESH = pl.DeviceIdType.MESH


def iota(shape, dim):
    return lax.broadcasted_iota(jnp.int32, shape, dim)


def kernel(
    n_e, n_a,
    greens, coupling, neighbours_in, counts_in, weights_in, offsets_in,
    sigma_out, phonon_out, current_out,
    neighbours, counts, weights, offsets, local_coupling, recv, framed, left, right, kron, sources, higher,
    sums, inter, pre, mine_p, got_p, mine_c, got_c,
    send_sem, recv_sem, own_sem, esend, erecv, psend, precv, csend, crecv,
):
    _, rows, all_atoms, cells = greens.shape
    slots, atoms = neighbours.shape
    edges = atoms * slots
    width = n_a * rows
    span = width + 2 * REACH
    planes = 2 * rows
    window = atoms + 2 * REACH
    halves = cells // LANES
    line = halves * atoms
    ei = lax.axis_index("energy")
    ai = lax.axis_index("atom")
    lower = ei > 0
    upper = ei < n_e - 1
    f32, bf16 = jnp.float32, jnp.bfloat16

    def ok(d):
        return {-1: lower, 1: upper}.get(d)

    def guarded(d, body):
        if d == 0:
            body()
        else:
            pl.when(ok(d))(body)

    coupling_copy = pltpu.make_async_copy(coupling, local_coupling, own_sem.at[1])
    coupling_copy.start()
    small = [
        pltpu.make_async_copy(source, target, own_sem.at[2 + i])
        for i, (source, target) in enumerate(
            [(neighbours_in, neighbours), (counts_in, counts),
             (weights_in, weights), (offsets_in, offsets)]
        )
    ]
    for copy in small:
        copy.start()

    barrier = pltpu.get_barrier_semaphore()

    def greet(e, a):
        pl.semaphore_signal(barrier, inc=1, device_id=(e, a), device_id_type=MESH)

    for d in (-1, 0, 1):
        for k in range(n_a):
            if d or k:
                guarded(d, lambda d=d, k=k: greet(ei + d, lax.rem(ai + k, n_a)))

    def greet_far(k, carry):
        other = lax.rem(ei + k, n_e)
        pl.when((other != ei - 1) & (other != ei + 1))(lambda: greet(other, ai))
        return carry

    lax.fori_loop(1, n_e, greet_far, 0)

    shape = (6 * width, 2 * span)
    row, col = iota(shape, 0), iota(shape, 1)
    kind = row // width
    half = (col // rows) % 2
    energy = (col // planes) * rows + col % rows
    distance = energy - row % width - REACH
    shift = jnp.where(kind == 0, distance, -distance)
    for copy in small:
        copy.wait()
    coef = jnp.zeros(shape, f32)
    for w in range(offsets.shape[0]):
        coef = coef + jnp.where(shift == offsets[w], weights[0, w], 0.0)
        coef = coef + jnp.where(shift == -offsets[w], weights[1, w], 0.0)
    middle = jnp.where((kind == 2) & (half == 1) & (distance == 0), 1.0, 0.0)
    above = jnp.where((kind >= 4) & (half == 0) & (energy - REACH == row - 4 * width), 1.0, 0.0)
    table = jnp.where((kind < 2) & (kind == half), coef, middle + above).astype(bf16)

    near = lower.astype(jnp.int32) + upper.astype(jnp.int32)
    pl.semaphore_wait(barrier, n_a - 1 + n_a * near + (n_e - 1 - near))

    def part(other):
        return greens.at[:, :, pl.ds(pl.multiple_of(other * atoms, atoms), atoms), :]

    def block_copy(d, k):
        other = lax.rem(ai + k, n_a)
        slot = (1 - d) * n_a + ai
        return pltpu.make_async_remote_copy(
            src_ref=part(other),
            dst_ref=recv.at[slot],
            send_sem=send_sem.at[(d + 1) * n_a + k],
            recv_sem=recv_sem.at[slot],
            device_id=(ei + d, other),
            device_id_type=MESH,
        )

    for k in range(n_a - 1, -1, -1):
        for d in (-1, 1, 0):
            if d or k:
                guarded(d, lambda d=d, k=k: block_copy(d, k).start())
    own = pltpu.make_async_copy(part(ai), recv.at[n_a + ai], own_sem.at[0])
    own.start()

    def clear(first):
        for k in range(n_a):
            recv[first + k] = jnp.zeros(recv.shape[1:], bf16)

    pl.when(jnp.logical_not(lower))(lambda: clear(0))
    pl.when(jnp.logical_not(upper))(lambda: clear(2 * n_a))

    big_row, big_col = iota((cells, cells), 0), iota((cells, cells), 1)
    same_block = (big_row // NO == big_col // NO).astype(f32).astype(bf16)
    same_place = (big_row // NO == big_col % NO).astype(f32).astype(bf16)
    coupling_copy.wait()
    flat = local_coupling[...].reshape(edges, cells).astype(f32)
    place = iota((edges, cells), 1) % NO

    def expand(j, carry):
        picked = jnp.where(place == j, flat, 0.0).astype(bf16)
        one = jnp.dot(picked, same_block, preferred_element_type=f32)
        two = jnp.dot(picked, same_place, preferred_element_type=f32)
        for h in range(halves):
            at = pl.ds(pl.multiple_of((h * NO + j) * edges, edges), edges)
            left[at, :] = one[:, h * LANES:(h + 1) * LANES]
            right[at, :] = two[:, h * LANES:(h + 1) * LANES]
        return carry

    lax.fori_loop(0, NO, expand, 0, unroll=4)

    def product(edge, carry):
        for h in range(halves):
            block = right[pl.ds(h * NO * edges + edge, NO, stride=edges), :]
            for j in range(NO):
                row = left[pl.ds((h * NO + j) * edges + edge, 1), :]
                kron[edge, j * NO:(j + 1) * NO, h * LANES:(h + 1) * LANES] = (
                    jnp.broadcast_to(row, (NO, LANES)) * block
                ).astype(bf16)
        return carry

    early = edges * 5 // 8
    lax.fori_loop(0, early, product, 0, unroll=4)

    own.wait()
    for d in (-1, 0, 1):
        for k in range(n_a):
            if d or k:
                def arrive(d=d, k=k):
                    slot = (d + 1) * n_a + lax.rem(ai + k, n_a)
                    pltpu.make_async_remote_copy(
                        src_ref=part(0),
                        dst_ref=recv.at[slot],
                        send_sem=send_sem.at[(d + 1) * n_a + k],
                        recv_sem=recv_sem.at[slot],
                        device_id=(ei + d, lax.rem(ai + k, n_a)),
                        device_id_type=MESH,
                    ).wait()
                guarded(d, arrive)

    def widen(position, carry):
        for plane in range(planes):
            value = recv[position, plane // rows, plane % rows].astype(f32)
            for h in range(halves):
                at = pl.multiple_of((position * planes + plane) * line + h * atoms, atoms)
                framed[pl.ds(at, atoms), :] = value[:, h * LANES:(h + 1) * LANES]
        return carry

    lax.fori_loop(0, 3 * n_a, widen, 0)

    def mix(t, carry):
        column = jnp.concatenate(
            [framed[pl.ds(h * atoms + t, 2 * span, stride=line), :] for h in range(halves)], axis=1
        ).astype(bf16)
        mixed = jnp.dot(table, column, preferred_element_type=f32).astype(bf16)
        sources[REACH + t] = mixed[0:4 * width]
        higher[t] = mixed[4 * width:]
        return carry

    has_left, has_right = ai > 0, ai < n_a - 1

    def edge_copy(side):
        start, landing = (REACH, REACH + atoms) if side == 0 else (atoms, 0)
        return pltpu.make_async_remote_copy(
            src_ref=sources.at[pl.ds(start, REACH)],
            dst_ref=sources.at[pl.ds(landing, REACH)],
            send_sem=esend.at[side],
            recv_sem=erecv.at[side],
            device_id=(ei, ai - 1 + 2 * side),
            device_id_type=MESH,
        )

    lax.fori_loop(0, REACH, mix, 0, unroll=4)
    pl.when(has_left)(lambda: edge_copy(0).start())
    lax.fori_loop(REACH, atoms, mix, 0, unroll=4)
    pl.when(has_right)(lambda: edge_copy(1).start())
    lax.fori_loop(early, edges, product, 0, unroll=4)
    pl.when(has_left)(lambda: edge_copy(0).wait_send())
    pl.when(has_right)(lambda: edge_copy(1).wait_send())
    pl.when(has_right)(lambda: edge_copy(0).wait_recv())
    pl.when(has_left)(lambda: edge_copy(1).wait_recv())

    first = ai * atoms - REACH
    both = 2 * width

    def atom_step(a, carry):
        total = jnp.zeros((both, cells), f32)
        bubbles = []
        for n in range(slots):
            place = jnp.clip(neighbours[n, a] - first, 0, window - 1)
            mixed = sources[place]
            result = jnp.dot(mixed, kron[a * slots + n], preferred_element_type=f32)
            live = jnp.where(n < counts[a], 1.0, 0.0)
            total = total + result[:both] * live
            bubbles.append(result[both:both + width])
        bubble = jnp.concatenate(bubbles, axis=0).astype(bf16)
        inter[pl.ds(pl.multiple_of(a * slots * width, slots * width), slots * width), 0:both] = (
            lax.dot_general(
                bubble, higher[a],
                (((1,), (1,)), ((), ())), preferred_element_type=f32,
            )
        )
        for h in range(halves):
            sums[pl.ds(h * both * atoms + a, both, stride=atoms), :] = total[
                :, h * LANES:(h + 1) * LANES
            ]
        return carry

    inter[...] = jnp.zeros(inter.shape, f32)
    lax.fori_loop(0, atoms, atom_step, 0, unroll=16)

    by_shift = jnp.zeros((edges, LANES), f32)
    for e in range(width):
        part = inter[pl.ds(e, edges, stride=width), :]
        by_shift = by_shift + pltpu.roll(part, (LANES - e - 1) % LANES, 1)
    mine_p[...] = by_shift.T[0:REACH, :]

    def phonon_copy(k):
        other = lax.rem(ei + k, n_e)
        return pltpu.make_async_remote_copy(
            src_ref=mine_p, dst_ref=got_p.at[ei],
            send_sem=psend.at[k], recv_sem=precv.at[ei],
            device_id=(other, ai), device_id_type=MESH,
        )

    def phonon_send(k, carry):
        phonon_copy(k).start()
        return carry

    lax.fori_loop(1, n_e, phonon_send, 0)

    place = iota((NO, cells), 1) % NO
    for e in range(width):
        sig, gre = [], []
        for s in (1, 0):
            parts = []
            for h in range(halves):
                at = (h * both + s * width + e) * atoms
                value = sums[at:at + atoms, :].astype(bf16)
                sigma_out[s, e, :, h * LANES:(h + 1) * LANES] = value
                parts.append(value)
            sig.append(jnp.concatenate(parts, axis=1))
        for g in range(2):
            base = ((n_a + e // rows) * planes + g * rows + e % rows) * line
            gre.append(jnp.concatenate(
                [framed[base + h * atoms:base + (h + 1) * atoms, :].astype(bf16) for h in range(halves)],
                axis=1,
            ))
        outer = lax.dot_general(
            jnp.concatenate(gre, axis=0), jnp.concatenate([sig[0], -sig[1]], axis=0),
            (((0,), (0,)), ((), ())), preferred_element_type=f32,
        )
        chosen = jnp.zeros((NO, cells), f32)
        for j in range(NO):
            chosen = jnp.where(place == j, outer[j * NO:(j + 1) * NO, :], chosen)
        pre[e * NO:(e + 1) * NO, :] = chosen
    value = pre[...]
    high = value.astype(bf16)
    low = (value - high.astype(f32)).astype(bf16)
    wide = jnp.dot(high, same_block, preferred_element_type=f32)
    wide = wide + jnp.dot(low, same_block, preferred_element_type=f32)
    keep = iota((width * NO, cells), 0) % NO == iota((width * NO, cells), 1) % NO
    wide = jnp.where(keep, wide, 0.0).reshape(width, NO, cells)
    share = jnp.sum(wide, axis=1) * (1.0 / math.sqrt(NO * all_atoms))
    mine_c[...] = share

    def current_copy(k):
        other = lax.rem(ai + k, n_a)
        return pltpu.make_async_remote_copy(
            src_ref=mine_c, dst_ref=got_c.at[ai],
            send_sem=csend.at[k], recv_sem=crecv.at[ai],
            device_id=(ei, other), device_id_type=MESH,
        )

    for k in range(1, n_a):
        current_copy(k).start()

    def phonon_wait(k, total):
        slot = lax.rem(ei + k, n_e)
        pltpu.make_async_remote_copy(
            src_ref=mine_p, dst_ref=got_p.at[slot],
            send_sem=psend.at[k], recv_sem=precv.at[slot],
            device_id=(slot, ai), device_id_type=MESH,
        ).wait()
        return total + got_p[slot]

    found = lax.fori_loop(1, n_e, phonon_wait, mine_p[...])
    count_w = offsets.shape[0]
    lanes = slots * count_w
    frequency = iota((REACH, lanes), 1) % count_w
    wanted = jnp.zeros((REACH, lanes), jnp.int32)
    for w in range(count_w):
        wanted = jnp.where(frequency == w, offsets[w], wanted)
    select = (wanted - 1 == iota((REACH, lanes), 0)).astype(f32)
    tall = found.T
    picked = jnp.zeros((edges, lanes), f32)
    for k in range(REACH):
        picked = picked + tall[:, k:k + 1] * select[k:k + 1, :]
    keep = iota((edges, lanes), 0) % slots == iota((edges, lanes), 1) // count_w
    picked = jnp.sum(jnp.where(keep, picked, 0.0).reshape(atoms, slots, lanes), axis=1)
    used = jnp.zeros((atoms, lanes), jnp.int32)
    which = iota((atoms, lanes), 0)
    for a in range(atoms):
        used = jnp.where(which == a, counts[a], used)
    live = iota((atoms, lanes), 1) // count_w < used
    phonon_out[...] = jnp.where(live, picked * (1.0 / math.sqrt(cells * width * n_e)), 0.0)

    total = mine_c[...]
    for k in range(1, n_a):
        slot = lax.rem(ai + k, n_a)
        pltpu.make_async_remote_copy(
            src_ref=mine_c, dst_ref=got_c.at[slot],
            send_sem=csend.at[k], recv_sem=crecv.at[slot],
            device_id=(ei, slot), device_id_type=MESH,
        ).wait()
        total = total + got_c[slot]
    own_rows = total[0:rows]
    for k in range(1, n_a):
        own_rows = jnp.where(ai == k, total[k * rows:(k + 1) * rows], own_rows)
    current_out[...] = own_rows


def hand_over(a, b, c, x, y, z):
    x[...] = a[...]
    y[...] = b[...]
    z[...] = c[...]


def shards(n_e, n_a, greens, coupling, neighbours, counts, phonon_weights, offsets):
    _, rows, all_atoms, cells = greens.shape
    atoms, slots = neighbours.shape
    edges = atoms * slots
    width = n_a * rows
    span = width + 2 * REACH
    window = atoms + 2 * REACH
    f32, bf16 = jnp.float32, jnp.bfloat16
    halves = cells // LANES
    vmem = pl.BlockSpec(memory_space=pltpu.VMEM)
    hbm = pl.BlockSpec(memory_space=pltpu.HBM)
    dma = pltpu.SemaphoreType.DMA
    results = pl.pallas_call(
        functools.partial(kernel, n_e, n_a),
        out_shape=(
            jax.ShapeDtypeStruct((2, width, atoms, cells), bf16),
            jax.ShapeDtypeStruct((atoms, slots * offsets.shape[0]), f32),
            jax.ShapeDtypeStruct((rows, cells), f32),
        ),
        in_specs=[hbm] * 6,
        out_specs=(vmem, vmem, vmem),
        scratch_shapes=[
            pltpu.SMEM((slots, atoms), jnp.int32),
            pltpu.SMEM(counts.shape, jnp.int32),
            pltpu.SMEM(phonon_weights.shape, f32),
            pltpu.SMEM(offsets.shape, jnp.int32),
            pltpu.VMEM(coupling.shape, bf16),
            pltpu.VMEM((3 * n_a, 2, rows, atoms, cells), bf16),
            pltpu.VMEM((2 * span * halves * atoms, LANES), f32),
            pltpu.VMEM((halves * NO * edges, LANES), f32),
            pltpu.VMEM((halves * NO * edges, LANES), f32),
            pltpu.VMEM((edges, cells, cells), bf16),
            pltpu.VMEM((window, 4 * width, cells), bf16),
            pltpu.VMEM((atoms, 2 * width, cells), bf16),
            pltpu.VMEM((halves * 2 * width * atoms, LANES), f32),
            pltpu.VMEM((edges * width, LANES), f32),
            pltpu.VMEM((width * NO, cells), f32),
            pltpu.VMEM((REACH, edges), f32),
            pltpu.VMEM((n_e, REACH, edges), f32),
            pltpu.VMEM((width, cells), f32),
            pltpu.VMEM((n_a, width, cells), f32),
            dma((3 * n_a,)), dma((3 * n_a,)), dma((6,)), dma((2,)), dma((2,)),
            dma((n_e,)), dma((n_e,)), dma((n_a,)), dma((n_a,)),
        ],
        compiler_params=pltpu.CompilerParams(
            collective_id=0, has_side_effects=True, vmem_limit_bytes=63 * 1024 * 1024
        ),
    )(greens, coupling, neighbours.T, counts, phonon_weights, offsets)
    return pl.pallas_call(
        hand_over,
        out_shape=tuple(jax.ShapeDtypeStruct(r.shape, r.dtype) for r in results),
        in_specs=[vmem] * 3,
        out_specs=(vmem,) * 3,
    )(*results)


def solution(mesh):
    placed = (
        P(None, ("energy", "atom"), None, None),
        P("atom", None, None),
        P("atom", None),
        P("atom"),
        P(),
        P(),
    )
    return jax.shard_map(
        functools.partial(shards, mesh.shape["energy"], mesh.shape["atom"]),
        mesh=mesh,
        in_specs=placed,
        out_specs=(P(None, "energy", "atom", None), P("atom", None), P(("energy", "atom"), None)),
        check_vma=False,
    )
```
